32 devices in a mesh: seq: 4 (over x, core), vocab: 8 (over z, y).
Axes of the slice: x: 2, y: 2, z: 4, core: 2. Of those that a mesh axis runs over, the one named last changes fastest.
Arguments:
- hidden: bfloat16 [1024, 4096], P('seq'), may hold values from -48 to 48
- head_weight: bfloat16 [4096, 16384], P('seq', 'vocab'), may hold values from -0.09375 to 0.09375
- queries: float32 [8, 16384], P(None, 'vocab'), may hold values from 0 to 1, as said below
- passage_lengths: int32 [16], replicated, may hold values from 1 to 192, 1024 in all
- pairing: int32 [16], replicated, may hold values from 0 to 7
- doc_freq: int32 [16384], P('vocab'), may hold values from 0 to 4194304
Outputs:
- grad_hidden: bfloat16 [1024, 4096], P('seq', 'vocab')
- losses: float32 [2], replicated
The draws below stay inside these ranges and needn't reach their ends.
Inputs may be any that keep to these rules, and one draw needn't show every extreme that they name: `queries`: entries are nonnegative.
All inputs are finite; a program needn't handle non-finite values.
Results may differ from the reference program's by a relative error of at most 0.0039.
Values may be sent and summed in bfloat16 or wider, within the bound.
A program may use at most 128 MiB of HBM per device.

```python
import math
import jax
import jax.numpy as jnp
import numpy as np
from jax import lax

D = 4096
VOC_DEV = 2048
DOCS = 4194304
VOCAB = 16384
TOKENS = 1024
PASSAGES = 16
QUERIES = 8
MOST = 192
N_VOCAB = 8


def draw_hidden(key, part):
    first_key = jax.random.fold_in(key, 0)
    values = jnp.clip(jax.random.normal(first_key, (TOKENS, D), jnp.float32), -6.0, 6.0)
    return values.astype(jnp.bfloat16)


def draw_queries(key, part):
    column = jnp.arange(VOCAB, dtype=jnp.float32)
    rising = 1.0 + 2.0 * column / (VOCAB - 1)
    spread = jax.random.uniform(key, (QUERIES, VOCAB), jnp.float32, 0.0, 2.0)
    return 0.6 / jnp.sqrt(float(VOCAB)) * rising[None, :] * spread


def draw_doc_freq(key, part):
    entry = jnp.arange(VOCAB, dtype=jnp.int32)
    upper = 1 + DOCS // VOCAB * (VOCAB - entry)
    return jax.random.randint(key, (VOCAB,), 0, upper, dtype=jnp.int32)


def touch_ends(drawn, key, low, high):
    spot = [jax.random.randint(jax.random.fold_in(key, axis), (), 0, length) for axis, length in enumerate(drawn.shape)]
    longest = drawn.shape.index(max(drawn.shape))
    beside = spot[:longest] + [(spot[longest] + 1) % drawn.shape[longest]] + spot[longest + 1:]
    return drawn.at[tuple(spot)].set(low).at[tuple(beside)].set(high)


def shard_levels(own_key, shape, cuts, smallest, top_value):
    gain, own = 1.0, jax.random.fold_in(own_key, 6)
    for axis_at, shards_of in cuts:
        draws = jnp.exp(jax.random.uniform(jax.random.fold_in(own, axis_at), (shards_of,), jnp.float32, smallest / len(cuts), top_value / len(cuts)))
        gain = gain * jnp.repeat(draws, shape[axis_at] // shards_of).reshape([-1 if axis == axis_at else 1 for axis in range(len(shape))])
    return gain


def split_up(amount, total, limit, lean):
    portions = [(1 << 20) // math.isqrt(standing ** lean) + 1 for standing in range(2, amount + 1)]
    rest, given = total - limit - (amount - 1), [1] * (amount - 1)
    while rest > 0:
        movable = [i for i in range(amount - 1) if given[i] < limit]
        mass, budget = sum([portions[i] for i in movable]), rest
        for i in movable:
            addition = min(limit - given[i], max(1, budget * portions[i] // mass), rest)
            given[i] = given[i] + addition
            rest = rest - addition
    return np.array([limit] + given)


def ragged(rng, count, total, most, skew):
    if count == 2:
        one = jax.random.randint(rng, (), max(1, total - most), min(most, total - 1) + 1)
        return jnp.stack([one, total - one])
    sizes = jnp.asarray(split_up(count, total, most, skew), jnp.int32)
    couples = (count - 1) // 2
    source_of, sink = sizes[1:1 + 2 * couples:2], sizes[2:2 + 2 * couples:2]
    room = jnp.minimum(source_of - 1, most - sink)
    passed = jax.random.randint(jax.random.fold_in(rng, 1), (couples,), 0, 1 << 20) % (room + 1)
    sizes = sizes.at[1:1 + 2 * couples:2].set(source_of - passed).at[2:2 + 2 * couples:2].set(sink + passed)
    return sizes[jax.random.permutation(jax.random.fold_in(rng, 2), count)]


def centred(stream_key, shape, width, bound, cuts=(), kind=jnp.bfloat16):
    entries = jax.random.normal(stream_key, shape, jnp.float32) * width
    if len(cuts) > 0:
        entries = shard_levels(stream_key, shape, cuts, -0.22, 0.18) * entries
    return jnp.clip(entries, min=-bound, max=bound).astype(kind)


def setup_inputs(seed: int = 0) -> dict:
    key_of = jax.random.split(jax.random.key(seed), 7)
    hidden = draw_hidden(jax.random.fold_in(key_of[6], 71), 0)
    head_weight = centred(key_of[1], (D, VOCAB), D ** -0.5, 0.09375, ((0, 4), (1, 8)))
    queries = draw_queries(jax.random.fold_in(key_of[6], 71), 0)
    passage_lengths = ragged(key_of[3], PASSAGES, TOKENS, MOST, 2).astype(jnp.int32)
    pairing = touch_ends(jax.random.randint(key_of[4], (PASSAGES,), 0, QUERIES), jax.random.fold_in(key_of[4], 1), 0, QUERIES - 1).astype(jnp.int32)
    doc_freq = draw_doc_freq(jax.random.fold_in(key_of[6], 71), 0)
    return dict(hidden=hidden, head_weight=head_weight, queries=queries, passage_lengths=passage_lengths, pairing=pairing, doc_freq=doc_freq)


sharpness = 8.0
loss_scale = 16384.0
flops_weight = 32.0
highest = lax.Precision.HIGHEST


def passage_members(passage_lengths, position):
    finish = jnp.cumsum(passage_lengths).astype(jnp.int32)
    starts = finish - passage_lengths
    inside = (position[None, :] >= starts[:, None]) & (position[None, :] < finish[:, None])
    return inside.astype(jnp.float32)


def saturate(logits):
    lifted = 1.0 + jax.nn.relu(logits)
    squared = lifted * lifted
    fourth = squared * squared
    return lifted, squared, fourth, fourth * fourth


def reference(hidden, head_weight, queries, passage_lengths, pairing, doc_freq):
    passages = passage_lengths.shape[0]
    query_count = queries.shape[0]
    vocab_total = head_weight.shape[1]
    position = jnp.arange(hidden.shape[0], dtype=jnp.int32)
    member = passage_members(passage_lengths, position)
    counts = passage_lengths.astype(jnp.float32)
    weights_all = jnp.log(1.0 + DOCS / (1.0 + doc_freq.astype(jnp.float32)))
    blocks = jnp.arange(N_VOCAB, dtype=jnp.int32)

    def forward_block(block_index):
        begin = (block_index * VOC_DEV).astype(jnp.int32)
        columns = lax.dynamic_slice_in_dim(head_weight, begin, VOC_DEV, 1)
        logits = jnp.dot(hidden, columns, preferred_element_type=jnp.float32)
        powered = saturate(logits)[3]
        totals = jnp.dot(member, powered, precision=highest)
        pooled = (jnp.log(totals) - jnp.log(counts)[:, None]) / sharpness
        col_mean = jnp.sum(pooled, axis=0) / passages
        weights_df = lax.dynamic_slice_in_dim(weights_all, begin, VOC_DEV, 0)
        query_cols = lax.dynamic_slice_in_dim(queries, begin, VOC_DEV, 1)
        return columns, logits, totals, pooled, col_mean, weights_df, query_cols

    def forward_step(state, block_index):
        scores, flops_sum = state
        columns, logits, totals, pooled, col_mean, weights_df, query_cols = forward_block(block_index)
        scores = scores + jnp.dot(query_cols, pooled.T, precision=highest)
        flops_sum = flops_sum + jnp.sum(weights_df * col_mean * col_mean)
        return (scores, flops_sum), None

    initial = (jnp.zeros((query_count, passages), jnp.float32), jnp.zeros((), jnp.float32))
    (scores, flops_sum), unused = lax.scan(forward_step, initial, blocks)
    flops_value = flops_sum / vocab_total
    onehot = (jnp.arange(query_count, dtype=jnp.int32)[:, None] == pairing[None, :]).astype(jnp.float32)
    peak_score = jnp.max(scores, axis=0)
    shifted = jnp.exp(scores - peak_score[None, :])
    denominator = jnp.sum(shifted, axis=0)
    log_total = peak_score + jnp.log(denominator)
    contrast = jnp.mean(log_total - jnp.sum(onehot * scores, axis=0))
    dscores = (shifted / denominator[None, :] - onehot) * (loss_scale / passages)
    flops_grad = loss_scale * flops_weight * 2.0 / (vocab_total * passages)

    def backward_step(gradient, block_index):
        columns, logits, totals, pooled, col_mean, weights_df, query_cols = forward_block(block_index)
        dpooled = jnp.dot(dscores.T, query_cols, precision=highest) + flops_grad * weights_df * col_mean
        factor = dpooled / totals
        spread = jnp.dot(member.T, factor, precision=highest)
        lifted, squared, fourth, powered = saturate(logits)
        seventh = fourth * squared * lifted
        dlogits = jnp.where(logits > 0, spread * seventh, 0.0).astype(jnp.bfloat16)
        gradient = gradient + lax.dot_general(dlogits, columns, (((1,), (1,)), ((), ())), preferred_element_type=jnp.float32)
        return gradient, None

    gradient, unused = lax.scan(backward_step, jnp.zeros(hidden.shape, jnp.float32), blocks)
    losses = jnp.stack([contrast, flops_value])
    return gradient.astype(jnp.bfloat16), losses
```

```python
import functools

import jax
import jax.numpy as jnp
from jax import lax
from jax.experimental import pallas as pl
from jax.experimental.pallas import tpu as pltpu
from jax.sharding import PartitionSpec as P

DOCS = 4194304

sharpness = 8.0
loss_scale = 16384.0
flops_weight = 32.0
highest = lax.Precision.HIGHEST
MESH = pl.DeviceIdType.MESH
PART = jnp.int16
LEVELS = 32767.0
f32 = jnp.float32
bf16 = jnp.bfloat16
TILE = 256


def powers(logits):
    lifted = 1.0 + jnp.maximum(logits, 0.0)
    squared = lifted * lifted
    fourth = squared * squared
    return lifted, squared, fourth


def rows_at(start, size, unit=128):
    return pl.ds(pl.multiple_of(start, unit), size)


def kernel(
    n_seq, n_voc, n_sem,
    hid_in, head_in, queries, len_row, pair_row, freq,
    out, losses,
    hid, head,    hidf, headp, psend, precv, scale_out, scale_in, lg, tot, totals_ref, factor_ref, pay, pay_in, sc, dl,
    g_send, g_recv, g_keep, h_send, h_recv, acc, fin_send, fin_recv, ss, rs, ls,
):
    s, v = lax.axis_index("seq"), lax.axis_index("vocab")
    chips = n_seq // 2
    x, k = s // 2, s % 2
    mate = x * 2 + (1 - k)
    tok, width = hid_in.shape
    blk, voc = head_in.shape
    half = voc // 2
    dcols = 2 * blk
    passages = len_row.shape[1]
    n_q = queries.shape[0]
    ratio = n_voc // n_seq
    pairs = ratio // 2
    odd, quad = v % 2, v // 2
    n2 = n_voc // 2
    piece = width // n_voc
    chunk = tok // 2
    count = [0]
    sent = []

    def sems(n=1):
        first = count[0]
        count[0] += n
        assert count[0] <= n_sem
        return first

    def copy(src, dst, slot, to, recv=None):
        return pltpu.make_async_remote_copy(
            src_ref=src, dst_ref=dst, send_sem=ss.at[slot],
            recv_sem=rs.at[slot if recv is None else recv],
            device_id=to, device_id_type=MESH,
        )

    def go(*args):
        c = copy(*args)
        c.start()
        sent.append(c)

    t_s, t_v = quad // pairs, s * ratio + 2 * (quad % pairs) + odd
    f_s, f_v = v // ratio, 2 * (s * pairs + (v % ratio) // 2) + odd
    moved = jnp.logical_or(t_s != s, t_v != v)

    barrier = pltpu.get_barrier_semaphore()
    for r in range(1, n_seq):
        pl.semaphore_signal(barrier, inc=1, device_id=((s + r) % n_seq, v), device_id_type=MESH)
    for r in range(1, n_voc):
        pl.semaphore_signal(barrier, inc=1, device_id=(s, (v + r) % n_voc), device_id_type=MESH)

    load_head = pltpu.make_async_copy(head_in, head, ls.at[0])
    load_hid = pltpu.make_async_copy(hid_in, hid, ls.at[1])
    load_head.start()
    load_hid.start()

    @pl.when(moved)
    def _():
        pl.semaphore_signal(barrier, inc=1, device_id=(f_s, f_v), device_id_type=MESH)
        pl.semaphore_wait(barrier, n_seq - 1 + n_voc)

    @pl.when(jnp.logical_not(moved))
    def _():
        pl.semaphore_wait(barrier, n_seq - 1 + n_voc - 1)

    near = (s, v + 1 - 2 * odd)
    hid_slots = {}
    for off in range(1, chips):
        to = lax.rem(x + off, chips)
        hid_slots[off] = sems()
        go(
            hid_in.at[rows_at(odd * chunk, chunk), rows_at(to * dcols, dcols)],
            hidf.at[rows_at(s * tok + odd * chunk, chunk)],
            hid_slots[off], (to * 2 + k, v),
        )
    own_cols = rows_at(x * dcols, dcols)
    head_slot, mine_slot = sems(), sems()
    go(head_in.at[:, rows_at((1 - k) * half, half)], headp, head_slot, (mate, v))
    go(hid_in.at[:, own_cols], hidf.at[rows_at(s * tok, tok)], mine_slot, (mate, v))

    def arrived(dst, slot):
        copy(dst, dst, slot, (mate, v)).wait_recv()

    def multiply(src, row, n_rows, base, put):
        def body(t, carry):
            left = src[rows_at(row, n_rows), rows_at(base + k * blk, blk)]
            right = src[rows_at(row, n_rows), rows_at(base + (1 - k) * blk, blk)]
            own = head[:, rows_at(k * half + t * TILE, TILE)]
            other = headp[:, rows_at(t * TILE, TILE)]
            res = jnp.dot(left, own, preferred_element_type=f32)
            put(t, res + jnp.dot(right, other, preferred_element_type=f32))
            return carry

        lax.fori_loop(0, half // TILE, body, 0)

    def put_lg(row):
        def put(t, res):
            lg[rows_at(row, res.shape[0]), rows_at(t * TILE, TILE)] = res

        return put

    load_head.wait()
    load_hid.wait()
    arrived(headp, head_slot)
    multiply(hid, 0, tok, x * dcols, put_lg(k * tok))
    arrived(hidf.at[rows_at(mate * tok, tok)], mine_slot)
    multiply(hidf, mate * tok, tok, 0, put_lg((1 - k) * tok))

    p_slots, scale_slots = {}, {}
    diagonal = lax.broadcasted_iota(jnp.int32, (chunk, chunk), 0) == lax.broadcasted_iota(
        jnp.int32, (chunk, chunk), 1
    )
    near_slots = {}
    for c in range(2):
        rank = odd if c == 0 else 1 - odd
        for off in range(1, chips):
            frm = lax.rem(x + chips - off, chips)
            block = hidf.at[rows_at((frm * 2 + k) * tok + rank * chunk, chunk)]
            fwd = sems()
            if c == 0:
                arrived(block, hid_slots[off])
                near_slots[off] = sems()
                go(block, block, near_slots[off], near)
            else:
                arrived(block, near_slots[off])
            go(block, block, fwd, (mate, v))
            for which in range(2):
                core = k if which == 0 else 1 - k
                if which == 1:
                    arrived(hidf.at[rows_at((frm * 2 + core) * tok + rank * chunk, chunk)], fwd)
                at = core * tok + rank * chunk

                def put(t, res, off=off, at=at, index=core * 2 + rank):
                    top = jnp.maximum(jnp.max(jnp.abs(res), axis=1, keepdims=True), 1e-30)
                    whole = jnp.round(res * (LEVELS / top)).astype(jnp.int32)
                    psend[off - 1, rows_at(at, chunk), rows_at(t * TILE, TILE)] = whole.astype(PART)
                    step = jnp.sum(
                        jnp.where(diagonal, top * (1.0 / LEVELS), 0.0), axis=0, keepdims=True
                    )
                    scale_out[off - 1, index, pl.ds(t, 1), :] = step

                multiply(hidf, (frm * 2 + core) * tok + rank * chunk, chunk, 0, put)
                p_slots[off, c, which] = sems()
                part = pl.ds(pl.multiple_of(at, 128), chunk)
                go(
                    psend.at[off - 1, part], precv.at[off - 1, part],
                    p_slots[off, c, which], (frm * 2 + k, v),
                )
                scale_slots[off, c, which] = sems()
                go(
                    scale_out.at[off - 1, core * 2 + rank], scale_in.at[off - 1, core * 2 + rank],
                    scale_slots[off, c, which], (frm * 2 + k, v),
                )
    for c in range(2):
        rank = odd if c == 0 else 1 - odd
        for off in range(1, chips):
            for which in range(2):
                core = k if which == 0 else 1 - k
                part = rows_at(core * tok + rank * chunk, chunk)
                arrived(precv.at[off - 1, part], p_slots[off, c, which])
                arrived(scale_in.at[off - 1, core * 2 + rank], scale_slots[off, c, which])

    square = (passages, passages)
    upto_row = lax.broadcasted_iota(jnp.int32, square, 0)
    upto_col = lax.broadcasted_iota(jnp.int32, square, 1)

    def upright(row):
        shown = jnp.where(upto_row == upto_col, row.astype(f32), 0.0)
        return jnp.sum(shown, axis=1, keepdims=True)

    counts = upright(len_row[...])
    len_col = counts.astype(jnp.int32)
    pair_col = upright(pair_row[...]).astype(jnp.int32)
    finish_col = jnp.sum(
        jnp.where(upto_col <= upto_row, len_row[...].astype(f32), 0.0), axis=1, keepdims=True
    ).astype(jnp.int32)
    finish_row = jnp.sum(
        jnp.where(upto_row <= upto_col, counts, 0.0), axis=0, keepdims=True
    ).astype(jnp.int32)
    here = 2 * tok
    place = x * here
    pos_row = place + lax.broadcasted_iota(jnp.int32, (passages, here), 1)
    member = jnp.logical_and(pos_row >= finish_col - len_col, pos_row < finish_col).astype(f32)

    def sum_tile(t, carry):
        cols = rows_at(t * TILE, TILE)
        for off in range(1, chips):
            for index in range(4):
                part = slice(index * chunk, (index + 1) * chunk)
                step = jnp.sum(
                    jnp.where(diagonal, scale_in[off - 1, index, pl.ds(t, 1), :], 0.0),
                    axis=1, keepdims=True,
                )
                whole = precv[off - 1, part, cols].astype(jnp.int32)
                lg[part, cols] += whole.astype(f32) * step
        logits = lg[:, cols]
        fourth = powers(logits)[2]
        tot[x, :, cols] = jnp.dot(
            member, fourth * fourth, precision=highest, preferred_element_type=f32
        )
        return carry

    lax.fori_loop(0, half // TILE, sum_tile, 0)
    base = sems(chips)
    for off in range(1, chips):
        to = lax.rem(x + off, chips)
        go(tot.at[x], tot.at[x], base + off, (to * 2 + k, v))
    for off in range(1, chips):
        frm = lax.rem(x + chips - off, chips)
        arrived(tot.at[frm], base + off)
    totals = tot[0]
    for c in range(1, chips):
        totals = totals + tot[c]
    totals_ref[...] = totals
    pooled = (jnp.log(totals) - jnp.log(counts)) / sharpness
    col_mean = jnp.sum(pooled, axis=0, keepdims=True) / passages
    freqs = freq[:, rows_at(k * half, half)].astype(f32)
    weights_df = jnp.log(1.0 + DOCS / (1.0 + freqs))
    vocab_total = voc * n_voc
    q_half = queries[:, rows_at(k * half, half)]
    pay[...] = jnp.zeros_like(pay)
    for i in range(n_q):
        pay[0:passages, i : i + 1] = jnp.sum(pooled * q_half[i : i + 1, :], axis=1, keepdims=True)
    pay[passages : passages + 1, 0:1] = jnp.sum(
        weights_df * col_mean * col_mean, axis=1, keepdims=True
    )
    slot = sems()
    go(pay, pay_in, slot, (mate, v))
    arrived(pay_in, slot)
    sc[v] = pay[...] + pay_in[...]
    out_base, in_base = sems(n_voc), sems(n_voc)
    for r in range(1, n_voc):
        go(sc.at[v], sc.at[v], out_base + r, (s, lax.rem(v + r, n_voc)), in_base + v)
    for r in range(1, n_voc):
        frm = lax.rem(v + r, n_voc)
        arrived(sc.at[frm], in_base + frm)
    everything = sc[0]
    for c in range(1, n_voc):
        everything = everything + sc[c]
    scores = everything[0:passages, 0:n_q]
    flops_value = everything[passages : passages + 1, 0:1] / vocab_total
    onehot = (lax.broadcasted_iota(jnp.int32, (passages, n_q), 1) == pair_col).astype(f32)
    peak = jnp.max(scores, axis=1, keepdims=True)
    shifted = jnp.exp(scores - peak)
    denominator = jnp.sum(shifted, axis=1, keepdims=True)
    each = peak + jnp.log(denominator) - jnp.sum(onehot * scores, axis=1, keepdims=True)
    contrast = jnp.sum(each, axis=0, keepdims=True) / passages
    lane = lax.broadcasted_iota(jnp.int32, losses.shape, 1)
    losses[...] = jnp.where(lane == 0, contrast, flops_value)
    dscores = (shifted / denominator - onehot) * (loss_scale / passages)
    flops_grad = loss_scale * flops_weight * 2.0 / (vocab_total * passages)
    dpooled = flops_grad * weights_df * col_mean
    for i in range(n_q):
        dpooled = dpooled + dscores[:, i : i + 1] * q_half[i : i + 1, :]
    factor_ref[...] = dpooled / totals_ref[...]

    dl_slots, mate_slots, fwd_slots = {}, {}, {}
    starts_row = finish_row - len_row[...]
    for c in range(2):
        pos_col = place + c * tok + lax.broadcasted_iota(jnp.int32, (tok, passages), 0)
        belongs = jnp.logical_and(pos_col >= starts_row, pos_col < finish_row).astype(f32)

        def spread_tile(t, carry, c=c, belongs=belongs):
            cols = rows_at(t * TILE, TILE)
            logits = lg[c * tok : (c + 1) * tok, cols]
            lifted, squared, fourth = powers(logits)
            spread = jnp.dot(
                belongs, factor_ref[:, cols], precision=highest, preferred_element_type=f32
            )
            grad = jnp.where(logits > 0, spread * (fourth * squared * lifted), 0.0)
            dl[k, rows_at(place + c * tok, tok), cols] = grad.astype(bf16)
            return carry

        lax.fori_loop(0, half // TILE, spread_tile, 0)
        rows = dl.at[k, rows_at(place + c * tok, tok)]
        for off in range(1, chips):
            to = lax.rem(x + off, chips)
            dl_slots[off, c] = sems()
            go(rows, rows, dl_slots[off, c], (to * 2 + k, v))
        mate_slots[c] = sems()
        go(rows, rows, mate_slots[c], (mate, v))

    step = min(piece, TILE)

    def grad_piece(row, j, put):
        def body(t, carry):
            wide = rows_at(j * piece + t * step, step)
            res = None
            for h in range(2):
                one = lax.dot_general(
                    dl[h, rows_at(row, tok), :], head[wide, h * half : (h + 1) * half],
                    (((1,), (1,)), ((), ())), preferred_element_type=f32,
                )
                res = one if res is None else res + one
            put(rows_at(t * step, step), res)
            return carry

        lax.fori_loop(0, piece // step, body, 0)

    g_slots, h_slots = {}, {}
    h_in = sems(n2)

    def blocks(off):
        frm = lax.rem(x + chips - off, chips)
        return [(off * 2 + c, frm * 2 + c) for c in range(2)]

    def second_level(o, block):
        for jj in range(pairs):
            arrived(g_recv.at[o, jj], g_slots[o, jj])
            both = g_keep[o, jj] + g_recv[o, jj].astype(f32)
            q = block * pairs + jj
            h_slots[o, jj] = sems()

            @pl.when(q == quad)
            def _():
                acc[...] = both

            @pl.when(q != quad)
            def _():
                h_send[o, jj] = both.astype(bf16)
                copy(
                    h_send.at[o, jj], h_recv.at[quad], h_slots[o, jj],
                    (s, 2 * q + odd), h_in + quad,
                ).start()

    waiting = []
    for off in range(chips):
        frm = lax.rem(x + chips - off, chips)
        for c in range(2):
            o, block = off * 2 + c, frm * 2 + c
            if off > 0:
                while len(waiting) > (1 if o < n_seq - 1 else 0):
                    second_level(*waiting.pop(0))
                rows = dl.at[k, rows_at(block * tok, tok)]
                arrived(rows, dl_slots[off, c])
                fwd_slots[off, c] = sems()
                go(rows, rows, fwd_slots[off, c], (mate, v))
            rows = dl.at[1 - k, rows_at(block * tok, tok)]
            arrived(rows, mate_slots[c] if off == 0 else fwd_slots[off, c])
            for jj in range(pairs):

                def put_send(cols, res, o=o, jj=jj):
                    g_send[o, jj, :, cols] = res.astype(bf16)

                def put_keep(cols, res, o=o, jj=jj):
                    g_keep[o, jj, :, cols] = res

                grad_piece(block * tok, 2 * jj + 1 - odd, put_send)
                g_slots[o, jj] = sems()
                go(g_send.at[o, jj], g_recv.at[o, jj], g_slots[o, jj], near)
                grad_piece(block * tok, 2 * jj + odd, put_keep)
            waiting.append((o, block))
    for entry in waiting:
        second_level(*entry)

    total = acc[...]
    for r in range(1, n2):
        frm = lax.rem(quad + r, n2)
        arrived(h_recv.at[frm], h_in + frm)
        total = total + h_recv[frm].astype(f32)
    fin_send[...] = total.astype(bf16)
    last = sems()

    @pl.when(moved)
    def _():
        c = copy(fin_send, fin_recv, last, (t_s, t_v))
        c.start()
        c.wait_recv()
        out[...] = fin_recv[...]
        c.wait_send()

    @pl.when(jnp.logical_not(moved))
    def _():
        out[...] = fin_send[...]

    for off in range(chips):
        for o, block in blocks(off):
            for jj in range(pairs):
                q = block * pairs + jj

                @pl.when(q != quad)
                def _():
                    copy(
                        h_send.at[o, jj], h_recv.at[quad], h_slots[o, jj],
                        (s, 2 * q + odd), h_in + quad,
                    ).wait_send()

    for c in sent:
        c.wait_send()


def per_device(n_seq, n_voc, hidden, head_weight, queries, passage_lengths, pairing, doc_freq):
    tok, width = hidden.shape
    blk, voc = head_weight.shape
    passages, n_q = passage_lengths.shape[0], queries.shape[0]
    chips, half, n2 = n_seq // 2, voc // 2, n_voc // 2
    pairs = n_voc // n_seq // 2
    piece = width // n_voc
    others = max(chips - 1, 1)
    n_sem = 32 + 20 * chips + 3 * n_voc + n2 + 2 * n_seq * pairs
    pad = passages + 8
    vmem = pltpu.VMEM
    scratch = [
        vmem((tok, width), bf16),
        vmem((blk, voc), bf16),
        vmem((n_seq * tok, 2 * blk), bf16),
        vmem((blk, half), bf16),
        vmem((others, 2 * tok, half), PART),
        vmem((others, 2 * tok, half), PART),
        vmem((others, 4, half // TILE, tok // 2), f32),
        vmem((others, 4, half // TILE, tok // 2), f32),
        vmem((2 * tok, half), f32),
        vmem((chips, passages, half), f32),
        vmem((passages, half), f32),
        vmem((passages, half), f32),
        vmem((pad, 128), f32),
        vmem((pad, 128), f32),
        vmem((n_voc, pad, 128), f32),
        vmem((2, n_seq * tok, half), bf16),
        vmem((n_seq, pairs, tok, piece), bf16),
        vmem((n_seq, pairs, tok, piece), bf16),
        vmem((n_seq, pairs, tok, piece), f32),
        vmem((n_seq, pairs, tok, piece), bf16),
        vmem((n2, tok, piece), bf16),
        vmem((tok, piece), f32),
        vmem((tok, piece), bf16),
        vmem((tok, piece), bf16),
        pltpu.SemaphoreType.DMA((n_sem,)),
        pltpu.SemaphoreType.DMA((n_sem,)),
        pltpu.SemaphoreType.DMA((2,)),
    ]
    spec = pl.BlockSpec(memory_space=pltpu.VMEM)
    grad, losses = pl.pallas_call(
        functools.partial(kernel, n_seq, n_voc, n_sem),
        out_shape=(
            jax.ShapeDtypeStruct((tok, piece), bf16),
            jax.ShapeDtypeStruct((1, 128), f32),
        ),
        in_specs=[pl.BlockSpec(memory_space=pl.ANY)] * 2 + [spec] * 4,
        out_specs=(spec, spec),
        scratch_shapes=scratch,
        compiler_params=pltpu.CompilerParams(
            collective_id=0, has_side_effects=True, vmem_limit_bytes=56 * 1024 * 1024
        ),
    )(
        hidden, head_weight, queries, passage_lengths[None, :], pairing[None, :],
        doc_freq[None, :],
    )
    return grad, losses[0, :2]


def solution(mesh):
    placed = (P("seq", None), P("seq", "vocab"), P(None, "vocab"), P(), P(), P("vocab"))
    return jax.shard_map(
        functools.partial(per_device, mesh.shape["seq"], mesh.shape["vocab"]),
        mesh=mesh, in_specs=placed, out_specs=(P("seq", "vocab"), P()), check_vma=False,
    )
```

```python
import functools

import jax
import jax.numpy as jnp
from jax import lax
from jax.experimental import pallas as pl
from jax.experimental.pallas import tpu as pltpu
from jax.sharding import PartitionSpec as P

DOCS = 4194304

sharpness = 8.0
loss_scale = 16384.0
flops_weight = 32.0
highest = lax.Precision.HIGHEST
MESH = pl.DeviceIdType.MESH
PART = jnp.int16
LEVELS = 32767.0
f32 = jnp.float32
bf16 = jnp.bfloat16
TILE = 256


def powers(logits):
    lifted = 1.0 + jnp.maximum(logits, 0.0)
    squared = lifted * lifted
    fourth = squared * squared
    return lifted, squared, fourth


def rows_at(start, size, unit=128):
    return pl.ds(pl.multiple_of(start, unit), size)


def kernel(
    n_seq, n_voc, n_sem,
    hid_in, head_in, queries, len_row, pair_row, freq,
    out, losses,
    hid, head,    hidf, headp, psend, precv, scale_out, scale_in, lg, tot, totals_ref, factor_ref, pay, pay_in, sc, dl,
    g_send, g_recv, g_keep, h_send, h_recv, fin_send, fin_recv, ss, rs, ls,
):
    s, v = lax.axis_index("seq"), lax.axis_index("vocab")
    chips = n_seq // 2
    x, k = s // 2, s % 2
    mate = x * 2 + (1 - k)
    tok, width = hid_in.shape
    blk, voc = head_in.shape
    half = voc // 2
    dcols = 2 * blk
    passages = len_row.shape[1]
    n_q = queries.shape[0]
    ratio = n_voc // n_seq
    pairs = ratio // 2
    odd, quad = v % 2, v // 2
    n2 = n_voc // 2
    piece = width // n_voc
    chunk = tok // 2
    count = [0]
    sent = []

    def sems(n=1):
        first = count[0]
        count[0] += n
        assert count[0] <= n_sem
        return first

    def copy(src, dst, slot, to, recv=None):
        return pltpu.make_async_remote_copy(
            src_ref=src, dst_ref=dst, send_sem=ss.at[slot],
            recv_sem=rs.at[slot if recv is None else recv],
            device_id=to, device_id_type=MESH,
        )

    def go(*args):
        c = copy(*args)
        c.start()
        sent.append(c)

    share = tok // n2
    home = v // ratio
    diagonal_one = home == s

    def target(block, jj):
        return block, s * ratio + 2 * jj + odd

    def source(r):
        return home, 2 * r + odd

    barrier = pltpu.get_barrier_semaphore()
    for r in range(1, n_seq):
        pl.semaphore_signal(barrier, inc=1, device_id=((s + r) % n_seq, v), device_id_type=MESH)
    for r in range(1, n_voc):
        pl.semaphore_signal(barrier, inc=1, device_id=(s, (v + r) % n_voc), device_id_type=MESH)

    load_head = pltpu.make_async_copy(head_in, head, ls.at[0])
    load_hid = pltpu.make_async_copy(hid_in, hid, ls.at[1])
    load_head.start()
    load_hid.start()

    for r in range(n2):

        @pl.when(jnp.logical_not(jnp.logical_and(diagonal_one, quad == r)))
        def _():
            pl.semaphore_signal(barrier, inc=1, device_id=source(r), device_id_type=MESH)

    peers = n_seq - 1 + n_voc - 1 + n2

    @pl.when(diagonal_one)
    def _():
        pl.semaphore_wait(barrier, peers - 1)

    @pl.when(jnp.logical_not(diagonal_one))
    def _():
        pl.semaphore_wait(barrier, peers)

    near = (s, v + 1 - 2 * odd)
    hid_slots = {}
    for off in range(1, chips):
        to = lax.rem(x + off, chips)
        hid_slots[off] = sems()
        go(
            hid_in.at[rows_at(odd * chunk, chunk), rows_at(to * dcols, dcols)],
            hidf.at[rows_at(s * tok + odd * chunk, chunk)],
            hid_slots[off], (to * 2 + k, v),
        )
    own_cols = rows_at(x * dcols, dcols)
    head_slot, mine_slot = sems(), sems()
    go(head_in.at[:, rows_at((1 - k) * half, half)], headp, head_slot, (mate, v))
    go(hid_in.at[:, own_cols], hidf.at[rows_at(s * tok, tok)], mine_slot, (mate, v))

    def arrived(dst, slot):
        copy(dst, dst, slot, (mate, v)).wait_recv()

    def multiply(src, row, n_rows, base, put):
        def body(t, carry):
            left = src[rows_at(row, n_rows), rows_at(base + k * blk, blk)]
            right = src[rows_at(row, n_rows), rows_at(base + (1 - k) * blk, blk)]
            own = head[:, rows_at(k * half + t * TILE, TILE)]
            other = headp[:, rows_at(t * TILE, TILE)]
            res = jnp.dot(left, own, preferred_element_type=f32)
            put(t, res + jnp.dot(right, other, preferred_element_type=f32))
            return carry

        lax.fori_loop(0, half // TILE, body, 0)

    def put_lg(row):
        def put(t, res):
            lg[rows_at(row, res.shape[0]), rows_at(t * TILE, TILE)] = res

        return put

    load_head.wait()
    load_hid.wait()
    arrived(headp, head_slot)
    multiply(hid, 0, tok, x * dcols, put_lg(k * tok))
    arrived(hidf.at[rows_at(mate * tok, tok)], mine_slot)
    multiply(hidf, mate * tok, tok, 0, put_lg((1 - k) * tok))

    p_slots, scale_slots = {}, {}
    diagonal = lax.broadcasted_iota(jnp.int32, (chunk, chunk), 0) == lax.broadcasted_iota(
        jnp.int32, (chunk, chunk), 1
    )
    near_slots = {}
    for c in range(2):
        rank = odd if c == 0 else 1 - odd
        for off in range(1, chips):
            frm = lax.rem(x + chips - off, chips)
            block = hidf.at[rows_at((frm * 2 + k) * tok + rank * chunk, chunk)]
            fwd = sems()
            if c == 0:
                arrived(block, hid_slots[off])
                near_slots[off] = sems()
                go(block, block, near_slots[off], near)
            else:
                arrived(block, near_slots[off])
            go(block, block, fwd, (mate, v))
            for which in range(2):
                core = k if which == 0 else 1 - k
                if which == 1:
                    arrived(hidf.at[rows_at((frm * 2 + core) * tok + rank * chunk, chunk)], fwd)
                at = core * tok + rank * chunk

                def put(t, res, off=off, at=at, index=core * 2 + rank):
                    top = jnp.maximum(jnp.max(jnp.abs(res), axis=1, keepdims=True), 1e-30)
                    whole = jnp.round(res * (LEVELS / top)).astype(jnp.int32)
                    psend[off - 1, rows_at(at, chunk), rows_at(t * TILE, TILE)] = whole.astype(PART)
                    step = jnp.sum(
                        jnp.where(diagonal, top * (1.0 / LEVELS), 0.0), axis=0, keepdims=True
                    )
                    scale_out[off - 1, index, pl.ds(t, 1), :] = step

                multiply(hidf, (frm * 2 + core) * tok + rank * chunk, chunk, 0, put)
                p_slots[off, c, which] = sems()
                part = pl.ds(pl.multiple_of(at, 128), chunk)
                go(
                    psend.at[off - 1, part], precv.at[off - 1, part],
                    p_slots[off, c, which], (frm * 2 + k, v),
                )
                scale_slots[off, c, which] = sems()
                go(
                    scale_out.at[off - 1, core * 2 + rank], scale_in.at[off - 1, core * 2 + rank],
                    scale_slots[off, c, which], (frm * 2 + k, v),
                )
    for c in range(2):
        rank = odd if c == 0 else 1 - odd
        for off in range(1, chips):
            for which in range(2):
                core = k if which == 0 else 1 - k
                part = rows_at(core * tok + rank * chunk, chunk)
                arrived(precv.at[off - 1, part], p_slots[off, c, which])
                arrived(scale_in.at[off - 1, core * 2 + rank], scale_slots[off, c, which])

    square = (passages, passages)
    upto_row = lax.broadcasted_iota(jnp.int32, square, 0)
    upto_col = lax.broadcasted_iota(jnp.int32, square, 1)

    def upright(row):
        shown = jnp.where(upto_row == upto_col, row.astype(f32), 0.0)
        return jnp.sum(shown, axis=1, keepdims=True)

    counts = upright(len_row[...])
    len_col = counts.astype(jnp.int32)
    pair_col = upright(pair_row[...]).astype(jnp.int32)
    finish_col = jnp.sum(
        jnp.where(upto_col <= upto_row, len_row[...].astype(f32), 0.0), axis=1, keepdims=True
    ).astype(jnp.int32)
    finish_row = jnp.sum(
        jnp.where(upto_row <= upto_col, counts, 0.0), axis=0, keepdims=True
    ).astype(jnp.int32)
    here = 2 * tok
    place = x * here
    pos_row = place + lax.broadcasted_iota(jnp.int32, (passages, here), 1)
    member = jnp.logical_and(pos_row >= finish_col - len_col, pos_row < finish_col).astype(f32)

    def sum_tile(t, carry):
        cols = rows_at(t * TILE, TILE)
        for off in range(1, chips):
            for index in range(4):
                part = slice(index * chunk, (index + 1) * chunk)
                step = jnp.sum(
                    jnp.where(diagonal, scale_in[off - 1, index, pl.ds(t, 1), :], 0.0),
                    axis=1, keepdims=True,
                )
                whole = precv[off - 1, part, cols].astype(jnp.int32)
                lg[part, cols] += whole.astype(f32) * step
        logits = lg[:, cols]
        fourth = powers(logits)[2]
        tot[x, :, cols] = jnp.dot(
            member, fourth * fourth, precision=highest, preferred_element_type=f32
        )
        return carry

    lax.fori_loop(0, half // TILE, sum_tile, 0)
    base = sems(chips)
    for off in range(1, chips):
        to = lax.rem(x + off, chips)
        go(tot.at[x], tot.at[x], base + off, (to * 2 + k, v))
    for off in range(1, chips):
        frm = lax.rem(x + chips - off, chips)
        arrived(tot.at[frm], base + off)
    totals = tot[0]
    for c in range(1, chips):
        totals = totals + tot[c]
    totals_ref[...] = totals
    pooled = (jnp.log(totals) - jnp.log(counts)) / sharpness
    col_mean = jnp.sum(pooled, axis=0, keepdims=True) / passages
    freqs = freq[:, rows_at(k * half, half)].astype(f32)
    weights_df = jnp.log(1.0 + DOCS / (1.0 + freqs))
    vocab_total = voc * n_voc
    q_half = queries[:, rows_at(k * half, half)]
    pay[...] = jnp.zeros_like(pay)
    for i in range(n_q):
        pay[0:passages, i : i + 1] = jnp.sum(pooled * q_half[i : i + 1, :], axis=1, keepdims=True)
    pay[passages : passages + 1, 0:1] = jnp.sum(
        weights_df * col_mean * col_mean, axis=1, keepdims=True
    )
    slot = sems()
    go(pay, pay_in, slot, (mate, v))
    arrived(pay_in, slot)
    sc[v] = pay[...] + pay_in[...]
    out_base, in_base = sems(n_voc), sems(n_voc)
    for r in range(1, n_voc):
        go(sc.at[v], sc.at[v], out_base + r, (s, lax.rem(v + r, n_voc)), in_base + v)
    for r in range(1, n_voc):
        frm = lax.rem(v + r, n_voc)
        arrived(sc.at[frm], in_base + frm)
    everything = sc[0]
    for c in range(1, n_voc):
        everything = everything + sc[c]
    scores = everything[0:passages, 0:n_q]
    flops_value = everything[passages : passages + 1, 0:1] / vocab_total
    onehot = (lax.broadcasted_iota(jnp.int32, (passages, n_q), 1) == pair_col).astype(f32)
    peak = jnp.max(scores, axis=1, keepdims=True)
    shifted = jnp.exp(scores - peak)
    denominator = jnp.sum(shifted, axis=1, keepdims=True)
    each = peak + jnp.log(denominator) - jnp.sum(onehot * scores, axis=1, keepdims=True)
    contrast = jnp.sum(each, axis=0, keepdims=True) / passages
    lane = lax.broadcasted_iota(jnp.int32, losses.shape, 1)
    losses[...] = jnp.where(lane == 0, contrast, flops_value)
    dscores = (shifted / denominator - onehot) * (loss_scale / passages)
    flops_grad = loss_scale * flops_weight * 2.0 / (vocab_total * passages)
    dpooled = flops_grad * weights_df * col_mean
    for i in range(n_q):
        dpooled = dpooled + dscores[:, i : i + 1] * q_half[i : i + 1, :]
    factor_ref[...] = dpooled / totals_ref[...]

    dl_slots, mate_slots, fwd_slots = {}, {}, {}
    starts_row = finish_row - len_row[...]
    for c in range(2):
        pos_col = place + c * tok + lax.broadcasted_iota(jnp.int32, (tok, passages), 0)
        belongs = jnp.logical_and(pos_col >= starts_row, pos_col < finish_row).astype(f32)

        def spread_tile(t, carry, c=c, belongs=belongs):
            cols = rows_at(t * TILE, TILE)
            logits = lg[c * tok : (c + 1) * tok, cols]
            lifted, squared, fourth = powers(logits)
            spread = jnp.dot(
                belongs, factor_ref[:, cols], precision=highest, preferred_element_type=f32
            )
            grad = jnp.where(logits > 0, spread * (fourth * squared * lifted), 0.0)
            dl[k, rows_at(place + c * tok, tok), cols] = grad.astype(bf16)
            return carry

        lax.fori_loop(0, half // TILE, spread_tile, 0)
        rows = dl.at[k, rows_at(place + c * tok, tok)]
        for off in range(1, chips):
            to = lax.rem(x + off, chips)
            dl_slots[off, c] = sems()
            go(rows, rows, dl_slots[off, c], (to * 2 + k, v))
        mate_slots[c] = sems()
        go(rows, rows, mate_slots[c], (mate, v))

    step = min(piece, TILE)

    def grad_piece(row, j, put):
        def body(t, carry):
            wide = rows_at(j * piece + t * step, step)
            res = None
            for h in range(2):
                one = lax.dot_general(
                    dl[h, rows_at(row, tok), :], head[wide, h * half : (h + 1) * half],
                    (((1,), (1,)), ((), ())), preferred_element_type=f32,
                )
                res = one if res is None else res + one
            put(rows_at(t * step, step), res)
            return carry

        lax.fori_loop(0, piece // step, body, 0)

    g_slots, h_slots, fin_slots = {}, {}, {}
    fin_in = sems(n2)
    mine = rows_at(quad * share, share, share)

    def second_level(o, block):
        for jj in range(pairs):
            arrived(g_recv.at[o, jj], g_slots[o, jj])
            both = g_keep[o, jj] + g_recv[o, jj].astype(f32)
            g_keep[o, jj] = both
            h_send[o, jj] = both.astype(bf16)
            h_slots[o, jj] = sems(n2)
            first = sems(n2)
            for r in range(1, n2):
                to = lax.rem(quad + r, n2)
                go(
                    h_send.at[o, jj, rows_at(to * share, share, share)], h_recv.at[o, jj, quad],
                    first + r, (s, 2 * to + odd), h_slots[o, jj] + quad,
                )

    def third_level(o, block):
        for jj in range(pairs):
            total = g_keep[o, jj, mine, :]
            for r in range(1, n2):
                frm = lax.rem(quad + r, n2)
                arrived(h_recv.at[o, jj, frm], h_slots[o, jj] + frm)
                total = total + h_recv[o, jj, frm].astype(f32)
            fin_send[o, jj] = total.astype(bf16)
            fin_slots[o, jj] = sems()
            t_s, t_v = target(block, jj)
            stays = jnp.logical_and(t_s == s, t_v == v)

            @pl.when(stays)
            def _():
                fin_recv[mine, :] = fin_send[o, jj]

            @pl.when(jnp.logical_not(stays))
            def _():
                deliver(o, jj, block).start()

    def deliver(o, jj, block):
        return copy(
            fin_send.at[o, jj], fin_recv.at[mine], fin_slots[o, jj],
            target(block, jj), fin_in + quad,
        )

    placed = []
    for off in range(chips):
        frm = lax.rem(x + chips - off, chips)
        for c in range(2):
            o, block = off * 2 + c, frm * 2 + c
            placed.append((o, block))
            if o >= 2:
                if o == 2:
                    second_level(*placed[0])
                else:
                    second_level(*placed[o - 2])
                    third_level(*placed[o - 3])
                    if o == n_seq - 1:
                        second_level(*placed[o - 1])
                        third_level(*placed[o - 2])
                rows = dl.at[k, rows_at(block * tok, tok)]
                arrived(rows, dl_slots[off, c])
                fwd_slots[off, c] = sems()
                go(rows, rows, fwd_slots[off, c], (mate, v))
            rows = dl.at[1 - k, rows_at(block * tok, tok)]
            arrived(rows, mate_slots[c] if off == 0 else fwd_slots[off, c])
            for jj in range(pairs):

                def put_send(cols, res, o=o, jj=jj):
                    g_send[o, jj, :, cols] = res.astype(bf16)

                def put_keep(cols, res, o=o, jj=jj):
                    g_keep[o, jj, :, cols] = res

                grad_piece(block * tok, 2 * jj + 1 - odd, put_send)
                g_slots[o, jj] = sems()
                go(g_send.at[o, jj], g_recv.at[o, jj], g_slots[o, jj], near)
                grad_piece(block * tok, 2 * jj + odd, put_keep)
    third_level(*placed[n_seq - 2])
    second_level(*placed[n_seq - 1])
    third_level(*placed[n_seq - 1])

    for r in range(n2):

        @pl.when(jnp.logical_not(jnp.logical_and(diagonal_one, quad == r)))
        def _():
            arrived(fin_recv.at[pl.ds(r * share, share)], fin_in + r)

    out[...] = fin_recv[...]
    for o, block in placed:
        for jj in range(pairs):
            t_s, t_v = target(block, jj)

            @pl.when(jnp.logical_not(jnp.logical_and(t_s == s, t_v == v)))
            def _():
                deliver(o, jj, block).wait_send()

    for c in sent:
        c.wait_send()


def per_device(n_seq, n_voc, hidden, head_weight, queries, passage_lengths, pairing, doc_freq):
    tok, width = hidden.shape
    blk, voc = head_weight.shape
    passages, n_q = passage_lengths.shape[0], queries.shape[0]
    chips, half, n2 = n_seq // 2, voc // 2, n_voc // 2
    pairs = n_voc // n_seq // 2
    piece = width // n_voc
    others = max(chips - 1, 1)
    n_sem = 32 + 20 * chips + 3 * n_voc + n2 + n_seq * pairs * (2 * n2 + 2)
    pad = passages + 8
    vmem = pltpu.VMEM
    scratch = [
        vmem((tok, width), bf16),
        vmem((blk, voc), bf16),
        vmem((n_seq * tok, 2 * blk), bf16),
        vmem((blk, half), bf16),
        vmem((others, 2 * tok, half), PART),
        vmem((others, 2 * tok, half), PART),
        vmem((others, 4, half // TILE, tok // 2), f32),
        vmem((others, 4, half // TILE, tok // 2), f32),
        vmem((2 * tok, half), f32),
        vmem((chips, passages, half), f32),
        vmem((passages, half), f32),
        vmem((passages, half), f32),
        vmem((pad, 128), f32),
        vmem((pad, 128), f32),
        vmem((n_voc, pad, 128), f32),
        vmem((2, n_seq * tok, half), bf16),
        vmem((n_seq, pairs, tok, piece), bf16),
        vmem((n_seq, pairs, tok, piece), bf16),
        vmem((n_seq, pairs, tok, piece), f32),
        vmem((n_seq, pairs, tok, piece), bf16),
        vmem((n_seq, pairs, n2, tok // n2, piece), bf16),
        vmem((n_seq, pairs, tok // n2, piece), bf16),
        vmem((tok, piece), bf16),
        pltpu.SemaphoreType.DMA((n_sem,)),
        pltpu.SemaphoreType.DMA((n_sem,)),
        pltpu.SemaphoreType.DMA((2,)),
    ]
    spec = pl.BlockSpec(memory_space=pltpu.VMEM)
    grad, losses = pl.pallas_call(
        functools.partial(kernel, n_seq, n_voc, n_sem),
        out_shape=(
            jax.ShapeDtypeStruct((tok, piece), bf16),
            jax.ShapeDtypeStruct((1, 128), f32),
        ),
        in_specs=[pl.BlockSpec(memory_space=pl.ANY)] * 2 + [spec] * 4,
        out_specs=(spec, spec),
        scratch_shapes=scratch,
        compiler_params=pltpu.CompilerParams(
            collective_id=0, has_side_effects=True, vmem_limit_bytes=56 * 1024 * 1024
        ),
    )(
        hidden, head_weight, queries, passage_lengths[None, :], pairing[None, :],
        doc_freq[None, :],
    )
    return grad, losses[0, :2]


def solution(mesh):
    placed = (P("seq", None), P("seq", "vocab"), P(None, "vocab"), P(), P(), P("vocab"))
    return jax.shard_map(
        functools.partial(per_device, mesh.shape["seq"], mesh.shape["vocab"]),
        mesh=mesh, in_specs=placed, out_specs=(P("seq", "vocab"), P()), check_vma=False,
    )
```

```python
import functools

import jax
import jax.numpy as jnp
from jax import lax
from jax.experimental import pallas as pl
from jax.experimental.pallas import tpu as pltpu
from jax.sharding import PartitionSpec as P

DOCS = 4194304

sharpness = 8.0
loss_scale = 16384.0
flops_weight = 32.0
highest = lax.Precision.HIGHEST
MESH = pl.DeviceIdType.MESH
PART = jnp.int16
LEVELS = 32767.0
f32 = jnp.float32
bf16 = jnp.bfloat16
TILE = 256


def powers(logits):
    lifted = 1.0 + jnp.maximum(logits, 0.0)
    squared = lifted * lifted
    fourth = squared * squared
    return lifted, squared, fourth


def rows_at(start, size, unit=128):
    return pl.ds(pl.multiple_of(start, unit), size)


def kernel(
    n_seq, n_voc, n_sem,
    hid_in, head_in, queries, len_row, pair_row, freq,
    out, losses,
    hid, head,    hidf, headp, psend, precv, scale_out, scale_in, lg, tot, totals_ref, factor_ref, pay, pay_in, sc, dl,
    g_send, g_recv, g_keep, h_send, h_recv, fin_send, fin_recv, ss, rs, ls,
):
    s, v = lax.axis_index("seq"), lax.axis_index("vocab")
    chips = n_seq // 2
    x, k = s // 2, s % 2
    mate = x * 2 + (1 - k)
    tok, width = hid_in.shape
    blk, voc = head_in.shape
    half = voc // 2
    dcols = 2 * blk
    passages = len_row.shape[1]
    n_q = queries.shape[0]
    ratio = n_voc // n_seq
    pairs = ratio // 2
    odd, quad = v % 2, v // 2
    n2 = n_voc // 2
    piece = width // n_voc
    chunk = tok // 2
    count = [0]
    sent = []

    def sems(n=1):
        first = count[0]
        count[0] += n
        assert count[0] <= n_sem
        return first

    def copy(src, dst, slot, to, recv=None):
        return pltpu.make_async_remote_copy(
            src_ref=src, dst_ref=dst, send_sem=ss.at[slot],
            recv_sem=rs.at[slot if recv is None else recv],
            device_id=to, device_id_type=MESH,
        )

    def go(*args):
        c = copy(*args)
        c.start()
        sent.append(c)

    share = tok // n2
    home = v // ratio
    diagonal_one = home == s

    def target(block, jj):
        return block, s * ratio + 2 * jj + odd

    def source(r):
        return home, 2 * r + odd

    barrier = pltpu.get_barrier_semaphore()
    for r in range(1, n_seq):
        pl.semaphore_signal(barrier, inc=1, device_id=((s + r) % n_seq, v), device_id_type=MESH)
    for r in range(1, n_voc):
        pl.semaphore_signal(barrier, inc=1, device_id=(s, (v + r) % n_voc), device_id_type=MESH)

    load_head = pltpu.make_async_copy(head_in, head, ls.at[0])
    load_hid = pltpu.make_async_copy(hid_in, hid, ls.at[1])
    load_head.start()
    load_hid.start()

    for r in range(n2):

        @pl.when(jnp.logical_not(jnp.logical_and(diagonal_one, quad == r)))
        def _():
            pl.semaphore_signal(barrier, inc=1, device_id=source(r), device_id_type=MESH)

    peers = n_seq - 1 + n_voc - 1 + n2

    @pl.when(diagonal_one)
    def _():
        pl.semaphore_wait(barrier, peers - 1)

    @pl.when(jnp.logical_not(diagonal_one))
    def _():
        pl.semaphore_wait(barrier, peers)

    near = (s, v + 1 - 2 * odd)
    hid_slots = {}
    for off in range(1, chips):
        to = lax.rem(x + off, chips)
        hid_slots[off] = sems()
        go(
            hid_in.at[rows_at(odd * chunk, chunk), rows_at(to * dcols, dcols)],
            hidf.at[rows_at(s * tok + odd * chunk, chunk)],
            hid_slots[off], (to * 2 + k, v),
        )
    own_cols = rows_at(x * dcols, dcols)
    head_slot, mine_slot = sems(), sems()
    go(head_in.at[:, rows_at((1 - k) * half, half)], headp, head_slot, (mate, v))
    go(hid_in.at[:, own_cols], hidf.at[rows_at(s * tok, tok)], mine_slot, (mate, v))

    def arrived(dst, slot):
        copy(dst, dst, slot, (mate, v)).wait_recv()

    def multiply(src, row, n_rows, base, put):
        def body(t, carry):
            left = src[rows_at(row, n_rows), rows_at(base + k * blk, blk)]
            right = src[rows_at(row, n_rows), rows_at(base + (1 - k) * blk, blk)]
            own = head[:, rows_at(k * half + t * TILE, TILE)]
            other = headp[:, rows_at(t * TILE, TILE)]
            res = jnp.dot(left, own, preferred_element_type=f32)
            put(t, res + jnp.dot(right, other, preferred_element_type=f32))
            return carry

        lax.fori_loop(0, half // TILE, body, 0)

    def put_lg(row):
        def put(t, res):
            lg[rows_at(row, res.shape[0]), rows_at(t * TILE, TILE)] = res

        return put

    load_head.wait()
    load_hid.wait()
    arrived(headp, head_slot)
    multiply(hid, 0, tok, x * dcols, put_lg(k * tok))
    arrived(hidf.at[rows_at(mate * tok, tok)], mine_slot)
    multiply(hidf, mate * tok, tok, 0, put_lg((1 - k) * tok))

    p_slots, scale_slots = {}, {}
    diagonal = lax.broadcasted_iota(jnp.int32, (chunk, chunk), 0) == lax.broadcasted_iota(
        jnp.int32, (chunk, chunk), 1
    )
    near_slots = {}
    for c in range(2):
        rank = odd if c == 0 else 1 - odd
        for off in range(1, chips):
            frm = lax.rem(x + chips - off, chips)
            block = hidf.at[rows_at((frm * 2 + k) * tok + rank * chunk, chunk)]
            fwd = sems()
            if c == 0:
                arrived(block, hid_slots[off])
                near_slots[off] = sems()
                go(block, block, near_slots[off], near)
            else:
                arrived(block, near_slots[off])
            go(block, block, fwd, (mate, v))
            for which in range(2):
                core = k if which == 0 else 1 - k
                if which == 1:
                    arrived(hidf.at[rows_at((frm * 2 + core) * tok + rank * chunk, chunk)], fwd)
                at = core * tok + rank * chunk

                def put(t, res, off=off, at=at, index=core * 2 + rank):
                    top = jnp.maximum(jnp.max(jnp.abs(res), axis=1, keepdims=True), 1e-30)
                    whole = jnp.round(res * (LEVELS / top)).astype(jnp.int32)
                    psend[off - 1, rows_at(at, chunk), rows_at(t * TILE, TILE)] = whole.astype(PART)
                    step = jnp.sum(
                        jnp.where(diagonal, top * (1.0 / LEVELS), 0.0), axis=0, keepdims=True
                    )
                    scale_out[off - 1, index, pl.ds(t, 1), :] = step

                multiply(hidf, (frm * 2 + core) * tok + rank * chunk, chunk, 0, put)
                p_slots[off, c, which] = sems()
                part = pl.ds(pl.multiple_of(at, 128), chunk)
                go(
                    psend.at[off - 1, part], precv.at[off - 1, part],
                    p_slots[off, c, which], (frm * 2 + k, v),
                )
                scale_slots[off, c, which] = sems()
                go(
                    scale_out.at[off - 1, core * 2 + rank], scale_in.at[off - 1, core * 2 + rank],
                    scale_slots[off, c, which], (frm * 2 + k, v),
                )
    for c in range(2):
        rank = odd if c == 0 else 1 - odd
        for off in range(1, chips):
            for which in range(2):
                core = k if which == 0 else 1 - k
                part = rows_at(core * tok + rank * chunk, chunk)
                arrived(precv.at[off - 1, part], p_slots[off, c, which])
                arrived(scale_in.at[off - 1, core * 2 + rank], scale_slots[off, c, which])

    square = (passages, passages)
    upto_row = lax.broadcasted_iota(jnp.int32, square, 0)
    upto_col = lax.broadcasted_iota(jnp.int32, square, 1)

    def upright(row):
        shown = jnp.where(upto_row == upto_col, row.astype(f32), 0.0)
        return jnp.sum(shown, axis=1, keepdims=True)

    counts = upright(len_row[...])
    len_col = counts.astype(jnp.int32)
    pair_col = upright(pair_row[...]).astype(jnp.int32)
    finish_col = jnp.sum(
        jnp.where(upto_col <= upto_row, len_row[...].astype(f32), 0.0), axis=1, keepdims=True
    ).astype(jnp.int32)
    finish_row = jnp.sum(
        jnp.where(upto_row <= upto_col, counts, 0.0), axis=0, keepdims=True
    ).astype(jnp.int32)
    here = 2 * tok
    place = x * here
    pos_row = place + lax.broadcasted_iota(jnp.int32, (passages, here), 1)
    member = jnp.logical_and(pos_row >= finish_col - len_col, pos_row < finish_col).astype(f32)

    def sum_tile(t, carry):
        cols = rows_at(t * TILE, TILE)
        for off in range(1, chips):
            for index in range(4):
                part = slice(index * chunk, (index + 1) * chunk)
                step = jnp.sum(
                    jnp.where(diagonal, scale_in[off - 1, index, pl.ds(t, 1), :], 0.0),
                    axis=1, keepdims=True,
                )
                whole = precv[off - 1, part, cols].astype(jnp.int32)
                lg[part, cols] += whole.astype(f32) * step
        logits = lg[:, cols]
        fourth = powers(logits)[2]
        tot[x, :, cols] = jnp.dot(
            member, fourth * fourth, precision=highest, preferred_element_type=f32
        )
        return carry

    lax.fori_loop(0, half // TILE, sum_tile, 0)
    base = sems(chips)
    for off in range(1, chips):
        to = lax.rem(x + off, chips)
        go(tot.at[x], tot.at[x], base + off, (to * 2 + k, v))
    for off in range(1, chips):
        frm = lax.rem(x + chips - off, chips)
        arrived(tot.at[frm], base + off)
    totals = tot[0]
    for c in range(1, chips):
        totals = totals + tot[c]
    totals_ref[...] = totals
    pooled = (jnp.log(totals) - jnp.log(counts)) / sharpness
    col_mean = jnp.sum(pooled, axis=0, keepdims=True) / passages
    freqs = freq[:, rows_at(k * half, half)].astype(f32)
    weights_df = jnp.log(1.0 + DOCS / (1.0 + freqs))
    vocab_total = voc * n_voc
    q_half = queries[:, rows_at(k * half, half)]
    pay[...] = jnp.zeros_like(pay)
    for i in range(n_q):
        pay[0:passages, i : i + 1] = jnp.sum(pooled * q_half[i : i + 1, :], axis=1, keepdims=True)
    pay[passages : passages + 1, 0:1] = jnp.sum(
        weights_df * col_mean * col_mean, axis=1, keepdims=True
    )
    slot = sems()
    go(pay, pay_in, slot, (mate, v))
    arrived(pay_in, slot)
    sc[v] = pay[...] + pay_in[...]
    out_base, in_base = sems(n_voc), sems(n_voc)
    for r in range(1, n_voc):
        go(sc.at[v], sc.at[v], out_base + r, (s, lax.rem(v + r, n_voc)), in_base + v)
    for r in range(1, n_voc):
        frm = lax.rem(v + r, n_voc)
        arrived(sc.at[frm], in_base + frm)
    everything = sc[0]
    for c in range(1, n_voc):
        everything = everything + sc[c]
    scores = everything[0:passages, 0:n_q]
    flops_value = everything[passages : passages + 1, 0:1] / vocab_total
    onehot = (lax.broadcasted_iota(jnp.int32, (passages, n_q), 1) == pair_col).astype(f32)
    peak = jnp.max(scores, axis=1, keepdims=True)
    shifted = jnp.exp(scores - peak)
    denominator = jnp.sum(shifted, axis=1, keepdims=True)
    each = peak + jnp.log(denominator) - jnp.sum(onehot * scores, axis=1, keepdims=True)
    contrast = jnp.sum(each, axis=0, keepdims=True) / passages
    lane = lax.broadcasted_iota(jnp.int32, losses.shape, 1)
    losses[...] = jnp.where(lane == 0, contrast, flops_value)
    dscores = (shifted / denominator - onehot) * (loss_scale / passages)
    flops_grad = loss_scale * flops_weight * 2.0 / (vocab_total * passages)
    dpooled = flops_grad * weights_df * col_mean
    for i in range(n_q):
        dpooled = dpooled + dscores[:, i : i + 1] * q_half[i : i + 1, :]
    factor_ref[...] = dpooled / totals_ref[...]

    dl_slots, mate_slots, fwd_slots = {}, {}, {}
    starts_row = finish_row - len_row[...]
    for c in range(2):
        pos_col = place + c * tok + lax.broadcasted_iota(jnp.int32, (tok, passages), 0)
        belongs = jnp.logical_and(pos_col >= starts_row, pos_col < finish_row).astype(f32)

        def spread_tile(t, carry, c=c, belongs=belongs):
            cols = rows_at(t * TILE, TILE)
            logits = lg[c * tok : (c + 1) * tok, cols]
            lifted, squared, fourth = powers(logits)
            spread = jnp.dot(
                belongs, factor_ref[:, cols], precision=highest, preferred_element_type=f32
            )
            grad = jnp.where(logits > 0, spread * (fourth * squared * lifted), 0.0)
            dl[k, rows_at(place + c * tok, tok), cols] = grad.astype(bf16)
            return carry

        lax.fori_loop(0, half // TILE, spread_tile, 0)
        rows = dl.at[k, rows_at(place + c * tok, tok)]
        for first in range(0, tok, chunk):
            some = dl.at[k, rows_at(place + c * tok + first, chunk)]
            for off in range(1, chips):
                to = lax.rem(x + off, chips)
                dl_slots[off, c, first] = sems()
                go(some, some, dl_slots[off, c, first], (to * 2 + k, v))
        mate_slots[c] = sems()
        go(rows, rows, mate_slots[c], (mate, v))

    step = min(piece, TILE)

    def grad_piece(row, n_rows, j, put):
        def body(t, carry):
            wide = rows_at(j * piece + t * step, step)
            res = None
            for h in range(2):
                one = lax.dot_general(
                    dl[h, rows_at(row, n_rows), :], head[wide, h * half : (h + 1) * half],
                    (((1,), (1,)), ((), ())), preferred_element_type=f32,
                )
                res = one if res is None else res + one
            put(rows_at(t * step, step), res)
            return carry

        lax.fori_loop(0, piece // step, body, 0)

    g_slots, h_slots, fin_slots = {}, {}, {}
    fin_in = sems(n2)
    mine = rows_at(quad * share, share, share)

    def second_level(o, block):
        for jj in range(pairs):
            for first, n_rows, slot in g_slots[o, jj]:
                arrived(g_recv.at[o, jj, pl.ds(first, n_rows)], slot)
            both = g_keep[o, jj] + g_recv[o, jj].astype(f32)
            g_keep[o, jj] = both
            h_send[o, jj] = both.astype(bf16)
            h_slots[o, jj] = sems(n2)
            first = sems(n2)
            for r in range(1, n2):
                to = lax.rem(quad + r, n2)
                go(
                    h_send.at[o, jj, rows_at(to * share, share, share)], h_recv.at[o, jj, quad],
                    first + r, (s, 2 * to + odd), h_slots[o, jj] + quad,
                )

    def third_level(o, block):
        for jj in range(pairs):
            total = g_keep[o, jj, mine, :]
            for r in range(1, n2):
                frm = lax.rem(quad + r, n2)
                arrived(h_recv.at[o, jj, frm], h_slots[o, jj] + frm)
                total = total + h_recv[o, jj, frm].astype(f32)
            fin_send[o, jj] = total.astype(bf16)
            fin_slots[o, jj] = sems()
            t_s, t_v = target(block, jj)
            stays = jnp.logical_and(t_s == s, t_v == v)

            @pl.when(stays)
            def _():
                fin_recv[mine, :] = fin_send[o, jj]

            @pl.when(jnp.logical_not(stays))
            def _():
                deliver(o, jj, block).start()

    def deliver(o, jj, block):
        return copy(
            fin_send.at[o, jj], fin_recv.at[mine], fin_slots[o, jj],
            target(block, jj), fin_in + quad,
        )

    placed = []
    for off in range(chips):
        frm = lax.rem(x + chips - off, chips)
        for c in range(2):
            o, block = off * 2 + c, frm * 2 + c
            placed.append((o, block))
            if o >= 2:
                if o == 2:
                    second_level(*placed[0])
                else:
                    second_level(*placed[o - 2])
                    third_level(*placed[o - 3])
                    if o == n_seq - 1:
                        second_level(*placed[o - 1])
                        third_level(*placed[o - 2])
            n_rows = tok if off == 0 else chunk
            for first in range(0, tok, n_rows):
                row = block * tok + first
                if off > 0:
                    some = dl.at[k, rows_at(row, n_rows)]
                    arrived(some, dl_slots[off, c, first])
                    fwd_slots[off, c, first] = sems()
                    go(some, some, fwd_slots[off, c, first], (mate, v))
                arrived(
                    dl.at[1 - k, rows_at(row, n_rows)],
                    mate_slots[c] if off == 0 else fwd_slots[off, c, first],
                )
                for jj in range(pairs):

                    def put_send(cols, res, o=o, jj=jj, first=first, n_rows=n_rows):
                        g_send[o, jj, first : first + n_rows, cols] = res.astype(bf16)

                    def put_keep(cols, res, o=o, jj=jj, first=first, n_rows=n_rows):
                        g_keep[o, jj, first : first + n_rows, cols] = res

                    part = pl.ds(first, n_rows)
                    grad_piece(row, n_rows, 2 * jj + 1 - odd, put_send)
                    slot = sems()
                    g_slots.setdefault((o, jj), []).append((first, n_rows, slot))
                    go(g_send.at[o, jj, part], g_recv.at[o, jj, part], slot, near)
                    grad_piece(row, n_rows, 2 * jj + odd, put_keep)
    third_level(*placed[n_seq - 2])
    second_level(*placed[n_seq - 1])
    third_level(*placed[n_seq - 1])

    for r in range(n2):

        @pl.when(jnp.logical_not(jnp.logical_and(diagonal_one, quad == r)))
        def _():
            arrived(fin_recv.at[pl.ds(r * share, share)], fin_in + r)

    out[...] = fin_recv[...]
    for o, block in placed:
        for jj in range(pairs):
            t_s, t_v = target(block, jj)

            @pl.when(jnp.logical_not(jnp.logical_and(t_s == s, t_v == v)))
            def _():
                deliver(o, jj, block).wait_send()

    for c in sent:
        c.wait_send()


def per_device(n_seq, n_voc, hidden, head_weight, queries, passage_lengths, pairing, doc_freq):
    tok, width = hidden.shape
    blk, voc = head_weight.shape
    passages, n_q = passage_lengths.shape[0], queries.shape[0]
    chips, half, n2 = n_seq // 2, voc // 2, n_voc // 2
    pairs = n_voc // n_seq // 2
    piece = width // n_voc
    others = max(chips - 1, 1)
    n_sem = 32 + 28 * chips + 2 * n_seq * pairs + 3 * n_voc + n2 + n_seq * pairs * (2 * n2 + 2)
    pad = passages + 8
    vmem = pltpu.VMEM
    scratch = [
        vmem((tok, width), bf16),
        vmem((blk, voc), bf16),
        vmem((n_seq * tok, 2 * blk), bf16),
        vmem((blk, half), bf16),
        vmem((others, 2 * tok, half), PART),
        vmem((others, 2 * tok, half), PART),
        vmem((others, 4, half // TILE, tok // 2), f32),
        vmem((others, 4, half // TILE, tok // 2), f32),
        vmem((2 * tok, half), f32),
        vmem((chips, passages, half), f32),
        vmem((passages, half), f32),
        vmem((passages, half), f32),
        vmem((pad, 128), f32),
        vmem((pad, 128), f32),
        vmem((n_voc, pad, 128), f32),
        vmem((2, n_seq * tok, half), bf16),
        vmem((n_seq, pairs, tok, piece), bf16),
        vmem((n_seq, pairs, tok, piece), bf16),
        vmem((n_seq, pairs, tok, piece), f32),
        vmem((n_seq, pairs, tok, piece), bf16),
        vmem((n_seq, pairs, n2, tok // n2, piece), bf16),
        vmem((n_seq, pairs, tok // n2, piece), bf16),
        vmem((tok, piece), bf16),
        pltpu.SemaphoreType.DMA((n_sem,)),
        pltpu.SemaphoreType.DMA((n_sem,)),
        pltpu.SemaphoreType.DMA((2,)),
    ]
    spec = pl.BlockSpec(memory_space=pltpu.VMEM)
    grad, losses = pl.pallas_call(
        functools.partial(kernel, n_seq, n_voc, n_sem),
        out_shape=(
            jax.ShapeDtypeStruct((tok, piece), bf16),
            jax.ShapeDtypeStruct((1, 128), f32),
        ),
        in_specs=[pl.BlockSpec(memory_space=pl.ANY)] * 2 + [spec] * 4,
        out_specs=(spec, spec),
        scratch_shapes=scratch,
        compiler_params=pltpu.CompilerParams(
            collective_id=0, has_side_effects=True, vmem_limit_bytes=56 * 1024 * 1024
        ),
    )(
        hidden, head_weight, queries, passage_lengths[None, :], pairing[None, :],
        doc_freq[None, :],
    )
    return grad, losses[0, :2]


def solution(mesh):
    placed = (P("seq", None), P("seq", "vocab"), P(None, "vocab"), P(), P(), P("vocab"))
    return jax.shard_map(
        functools.partial(per_device, mesh.shape["seq"], mesh.shape["vocab"]),
        mesh=mesh, in_specs=placed, out_specs=(P("seq", "vocab"), P()), check_vma=False,
    )
```

```python
import functools

import jax
import jax.numpy as jnp
from jax import lax
from jax.experimental import pallas as pl
from jax.experimental.pallas import tpu as pltpu
from jax.sharding import PartitionSpec as P

DOCS = 4194304

sharpness = 8.0
loss_scale = 16384.0
flops_weight = 32.0
highest = lax.Precision.HIGHEST
MESH = pl.DeviceIdType.MESH
PART = jnp.int16
LEVELS = 32767.0
f32 = jnp.float32
bf16 = jnp.bfloat16
TILE = 256


def powers(logits):
    lifted = 1.0 + jnp.maximum(logits, 0.0)
    squared = lifted * lifted
    fourth = squared * squared
    return lifted, squared, fourth


def rows_at(start, size, unit=128):
    return pl.ds(pl.multiple_of(start, unit), size)


def kernel(
    n_seq, n_voc, n_sem,
    hid_in, head_in, queries, len_row, pair_row, freq,
    out, losses,
    hid, head,    hidf, headp, psend, precv, scale_out, scale_in, lg, tot, totals_ref, factor_ref, pay, pay_in, sc, dl,
    g_send, g_recv, g_keep, h_send, h_recv, fin_send, fin_recv, ss, rs, ls,
):
    s, v = lax.axis_index("seq"), lax.axis_index("vocab")
    chips = n_seq // 2
    x, k = s // 2, s % 2
    mate = x * 2 + (1 - k)
    tok, width = hid_in.shape
    blk, voc = head_in.shape
    half = voc // 2
    dcols = 2 * blk
    passages = len_row.shape[1]
    n_q = queries.shape[0]
    ratio = n_voc // n_seq
    pairs = ratio // 2
    odd, quad = v % 2, v // 2
    n2 = n_voc // 2
    piece = width // n_voc
    chunk = tok // 2
    count = [0]
    sent = []

    def sems(n=1):
        first = count[0]
        count[0] += n
        assert count[0] <= n_sem
        return first

    def copy(src, dst, slot, to, recv=None):
        return pltpu.make_async_remote_copy(
            src_ref=src, dst_ref=dst, send_sem=ss.at[slot],
            recv_sem=rs.at[slot if recv is None else recv],
            device_id=to, device_id_type=MESH,
        )

    def go(*args):
        c = copy(*args)
        c.start()
        sent.append(c)

    share = tok // n2
    home = v // ratio
    diagonal_one = home == s

    def target(block, jj):
        return block, s * ratio + 2 * jj + odd

    def source(r):
        return home, 2 * r + odd

    barrier = pltpu.get_barrier_semaphore()
    for r in range(1, n_seq):
        pl.semaphore_signal(barrier, inc=1, device_id=((s + r) % n_seq, v), device_id_type=MESH)
    for r in range(1, n_voc):
        pl.semaphore_signal(barrier, inc=1, device_id=(s, (v + r) % n_voc), device_id_type=MESH)

    load_head = pltpu.make_async_copy(head_in, head, ls.at[0])
    load_hid = pltpu.make_async_copy(hid_in, hid, ls.at[1])
    load_head.start()
    load_hid.start()

    for r in range(n2):

        @pl.when(jnp.logical_not(jnp.logical_and(diagonal_one, quad == r)))
        def _():
            pl.semaphore_signal(barrier, inc=1, device_id=source(r), device_id_type=MESH)

    peers = n_seq - 1 + n_voc - 1 + n2

    @pl.when(diagonal_one)
    def _():
        pl.semaphore_wait(barrier, peers - 1)

    @pl.when(jnp.logical_not(diagonal_one))
    def _():
        pl.semaphore_wait(barrier, peers)

    near = (s, v + 1 - 2 * odd)
    hid_slots = {}
    for off in range(1, chips):
        to = lax.rem(x + off, chips)
        hid_slots[off] = sems()
        go(
            hid_in.at[rows_at(odd * chunk, chunk), rows_at(to * dcols, dcols)],
            hidf.at[rows_at(s * tok + odd * chunk, chunk)],
            hid_slots[off], (to * 2 + k, v),
        )
    own_cols = rows_at(x * dcols, dcols)
    head_slot, mine_slot = sems(), sems()
    go(head_in.at[:, rows_at((1 - k) * half, half)], headp, head_slot, (mate, v))
    go(hid_in.at[:, own_cols], hidf.at[rows_at(s * tok, tok)], mine_slot, (mate, v))

    def arrived(dst, slot):
        copy(dst, dst, slot, (mate, v)).wait_recv()

    def multiply(src, row, n_rows, base, put):
        def body(t, carry):
            left = src[rows_at(row, n_rows), rows_at(base + k * blk, blk)]
            right = src[rows_at(row, n_rows), rows_at(base + (1 - k) * blk, blk)]
            own = head[:, rows_at(k * half + t * TILE, TILE)]
            other = headp[:, rows_at(t * TILE, TILE)]
            res = jnp.dot(left, own, preferred_element_type=f32)
            put(t, res + jnp.dot(right, other, preferred_element_type=f32))
            return carry

        lax.fori_loop(0, half // TILE, body, 0)

    def put_lg(row):
        def put(t, res):
            lg[rows_at(row, res.shape[0]), rows_at(t * TILE, TILE)] = res

        return put

    load_head.wait()
    load_hid.wait()
    arrived(headp, head_slot)
    multiply(hid, 0, tok, x * dcols, put_lg(k * tok))
    arrived(hidf.at[rows_at(mate * tok, tok)], mine_slot)
    multiply(hidf, mate * tok, tok, 0, put_lg((1 - k) * tok))

    p_slots, scale_slots = {}, {}
    diagonal = lax.broadcasted_iota(jnp.int32, (chunk, chunk), 0) == lax.broadcasted_iota(
        jnp.int32, (chunk, chunk), 1
    )
    near_slots = {}
    for c in range(2):
        rank = odd if c == 0 else 1 - odd
        for off in range(1, chips):
            frm = lax.rem(x + chips - off, chips)
            block = hidf.at[rows_at((frm * 2 + k) * tok + rank * chunk, chunk)]
            fwd = sems()
            if c == 0:
                arrived(block, hid_slots[off])
                near_slots[off] = sems()
                go(block, block, near_slots[off], near)
            else:
                arrived(block, near_slots[off])
            go(block, block, fwd, (mate, v))
            for which in range(2):
                core = k if which == 0 else 1 - k
                if which == 1:
                    arrived(hidf.at[rows_at((frm * 2 + core) * tok + rank * chunk, chunk)], fwd)
                at = core * tok + rank * chunk

                def put(t, res, off=off, at=at, index=core * 2 + rank):
                    top = jnp.maximum(jnp.max(jnp.abs(res), axis=1, keepdims=True), 1e-30)
                    whole = jnp.round(res * (LEVELS / top)).astype(jnp.int32)
                    psend[off - 1, rows_at(at, chunk), rows_at(t * TILE, TILE)] = whole.astype(PART)
                    step = jnp.sum(
                        jnp.where(diagonal, top * (1.0 / LEVELS), 0.0), axis=0, keepdims=True
                    )
                    scale_out[off - 1, index, pl.ds(t, 1), :] = step

                multiply(hidf, (frm * 2 + core) * tok + rank * chunk, chunk, 0, put)
                p_slots[off, c, which] = sems()
                part = pl.ds(pl.multiple_of(at, 128), chunk)
                go(
                    psend.at[off - 1, part], precv.at[off - 1, part],
                    p_slots[off, c, which], (frm * 2 + k, v),
                )
                scale_slots[off, c, which] = sems()
                go(
                    scale_out.at[off - 1, core * 2 + rank], scale_in.at[off - 1, core * 2 + rank],
                    scale_slots[off, c, which], (frm * 2 + k, v),
                )
    for c in range(2):
        rank = odd if c == 0 else 1 - odd
        for off in range(1, chips):
            for which in range(2):
                core = k if which == 0 else 1 - k
                part = rows_at(core * tok + rank * chunk, chunk)
                arrived(precv.at[off - 1, part], p_slots[off, c, which])
                arrived(scale_in.at[off - 1, core * 2 + rank], scale_slots[off, c, which])

    square = (passages, passages)
    upto_row = lax.broadcasted_iota(jnp.int32, square, 0)
    upto_col = lax.broadcasted_iota(jnp.int32, square, 1)

    def upright(row):
        shown = jnp.where(upto_row == upto_col, row.astype(f32), 0.0)
        return jnp.sum(shown, axis=1, keepdims=True)

    counts = upright(len_row[...])
    len_col = counts.astype(jnp.int32)
    pair_col = upright(pair_row[...]).astype(jnp.int32)
    finish_col = jnp.sum(
        jnp.where(upto_col <= upto_row, len_row[...].astype(f32), 0.0), axis=1, keepdims=True
    ).astype(jnp.int32)
    finish_row = jnp.sum(
        jnp.where(upto_row <= upto_col, counts, 0.0), axis=0, keepdims=True
    ).astype(jnp.int32)
    here = 2 * tok
    place = x * here
    pos_row = place + lax.broadcasted_iota(jnp.int32, (passages, here), 1)
    member = jnp.logical_and(pos_row >= finish_col - len_col, pos_row < finish_col).astype(f32)

    def sum_tile(t, carry):
        cols = rows_at(t * TILE, TILE)
        for off in range(1, chips):
            for index in range(4):
                part = slice(index * chunk, (index + 1) * chunk)
                step = jnp.sum(
                    jnp.where(diagonal, scale_in[off - 1, index, pl.ds(t, 1), :], 0.0),
                    axis=1, keepdims=True,
                )
                whole = precv[off - 1, part, cols].astype(jnp.int32)
                lg[part, cols] += whole.astype(f32) * step
        logits = lg[:, cols]
        fourth = powers(logits)[2]
        tot[x, :, cols] = jnp.dot(
            member, fourth * fourth, precision=highest, preferred_element_type=f32
        )
        return carry

    lax.fori_loop(0, half // TILE, sum_tile, 0)
    base = sems(chips)
    for off in range(1, chips):
        to = lax.rem(x + off, chips)
        go(tot.at[x], tot.at[x], base + off, (to * 2 + k, v))
    for off in range(1, chips):
        frm = lax.rem(x + chips - off, chips)
        arrived(tot.at[frm], base + off)
    totals = tot[0]
    for c in range(1, chips):
        totals = totals + tot[c]
    totals_ref[...] = totals
    pooled = (jnp.log(totals) - jnp.log(counts)) / sharpness
    col_mean = jnp.sum(pooled, axis=0, keepdims=True) / passages
    freqs = freq[:, rows_at(k * half, half)].astype(f32)
    weights_df = jnp.log(1.0 + DOCS / (1.0 + freqs))
    vocab_total = voc * n_voc
    q_half = queries[:, rows_at(k * half, half)]
    pay[...] = jnp.zeros_like(pay)
    for i in range(n_q):
        pay[0:passages, i : i + 1] = jnp.sum(pooled * q_half[i : i + 1, :], axis=1, keepdims=True)
    pay[passages : passages + 1, 0:1] = jnp.sum(
        weights_df * col_mean * col_mean, axis=1, keepdims=True
    )
    slot = sems()
    go(pay, pay_in, slot, (mate, v))
    arrived(pay_in, slot)
    sc[v] = pay[...] + pay_in[...]
    out_base, in_base = sems(n_voc), sems(n_voc)
    for r in range(1, n_voc):
        go(sc.at[v], sc.at[v], out_base + r, (s, lax.rem(v + r, n_voc)), in_base + v)
    for r in range(1, n_voc):
        frm = lax.rem(v + r, n_voc)
        arrived(sc.at[frm], in_base + frm)
    everything = sc[0]
    for c in range(1, n_voc):
        everything = everything + sc[c]
    scores = everything[0:passages, 0:n_q]
    flops_value = everything[passages : passages + 1, 0:1] / vocab_total
    onehot = (lax.broadcasted_iota(jnp.int32, (passages, n_q), 1) == pair_col).astype(f32)
    peak = jnp.max(scores, axis=1, keepdims=True)
    shifted = jnp.exp(scores - peak)
    denominator = jnp.sum(shifted, axis=1, keepdims=True)
    each = peak + jnp.log(denominator) - jnp.sum(onehot * scores, axis=1, keepdims=True)
    contrast = jnp.sum(each, axis=0, keepdims=True) / passages
    lane = lax.broadcasted_iota(jnp.int32, losses.shape, 1)
    losses[...] = jnp.where(lane == 0, contrast, flops_value)
    dscores = (shifted / denominator - onehot) * (loss_scale / passages)
    flops_grad = loss_scale * flops_weight * 2.0 / (vocab_total * passages)
    dpooled = flops_grad * weights_df * col_mean
    for i in range(n_q):
        dpooled = dpooled + dscores[:, i : i + 1] * q_half[i : i + 1, :]
    factor_ref[...] = dpooled / totals_ref[...]

    dl_slots, mate_slots, fwd_slots = {}, {}, {}
    starts_row = finish_row - len_row[...]
    for c in range(2):
        pos_col = place + c * tok + lax.broadcasted_iota(jnp.int32, (tok, passages), 0)
        belongs = jnp.logical_and(pos_col >= starts_row, pos_col < finish_row).astype(f32)

        def spread_tile(t, carry, c=c, belongs=belongs):
            cols = rows_at(t * TILE, TILE)
            logits = lg[c * tok : (c + 1) * tok, cols]
            lifted, squared, fourth = powers(logits)
            spread = jnp.dot(
                belongs, factor_ref[:, cols], precision=highest, preferred_element_type=f32
            )
            grad = jnp.where(logits > 0, spread * (fourth * squared * lifted), 0.0)
            dl[k, rows_at(place + c * tok, tok), cols] = grad.astype(bf16)
            return carry

        lax.fori_loop(0, half // TILE, spread_tile, 0)
        rows = dl.at[k, rows_at(place + c * tok, tok)]
        for off in range(1, chips):
            to = lax.rem(x + off, chips)
            dl_slots[off, c] = sems()
            go(rows, rows, dl_slots[off, c], (to * 2 + k, v))
        mate_slots[c] = sems()
        go(rows, rows, mate_slots[c], (mate, v))

    step = min(piece, 2 * TILE)

    def grad_piece(row, j, put):
        def body(t, carry):
            wide = rows_at(j * piece + t * step, step)
            res = None
            for h in range(2):
                one = lax.dot_general(
                    dl[h, rows_at(row, tok), :], head[wide, h * half : (h + 1) * half],
                    (((1,), (1,)), ((), ())), preferred_element_type=f32,
                )
                res = one if res is None else res + one
            put(rows_at(t * step, step), res)
            return carry

        lax.fori_loop(0, piece // step, body, 0)

    g_slots, h_slots, fin_slots = {}, {}, {}
    fin_in = sems(n2)
    mine = rows_at(quad * share, share, share)

    def second_level(o, block):
        for jj in range(pairs):
            arrived(g_recv.at[o, jj], g_slots[o, jj])
            both = g_keep[o, jj] + g_recv[o, jj].astype(f32)
            g_keep[o, jj] = both
            h_send[o, jj] = both.astype(bf16)
            h_slots[o, jj] = sems(n2)
            first = sems(n2)
            for r in range(1, n2):
                to = lax.rem(quad + r, n2)
                go(
                    h_send.at[o, jj, rows_at(to * share, share, share)], h_recv.at[o, jj, quad],
                    first + r, (s, 2 * to + odd), h_slots[o, jj] + quad,
                )

    def third_level(o, block):
        for jj in range(pairs):
            total = g_keep[o, jj, mine, :]
            for r in range(1, n2):
                frm = lax.rem(quad + r, n2)
                arrived(h_recv.at[o, jj, frm], h_slots[o, jj] + frm)
                total = total + h_recv[o, jj, frm].astype(f32)
            fin_send[o, jj] = total.astype(bf16)
            fin_slots[o, jj] = sems()
            t_s, t_v = target(block, jj)
            stays = jnp.logical_and(t_s == s, t_v == v)

            @pl.when(stays)
            def _():
                fin_recv[mine, :] = fin_send[o, jj]

            @pl.when(jnp.logical_not(stays))
            def _():
                deliver(o, jj, block).start()

    def deliver(o, jj, block):
        return copy(
            fin_send.at[o, jj], fin_recv.at[mine], fin_slots[o, jj],
            target(block, jj), fin_in + quad,
        )

    placed = []
    for off in range(chips):
        frm = lax.rem(x + chips - off, chips)
        for c in range(2):
            o, block = off * 2 + c, frm * 2 + c
            placed.append((o, block))
            if o >= 2:
                if o == 2:
                    second_level(*placed[0])
                else:
                    second_level(*placed[o - 2])
                    third_level(*placed[o - 3])
                    if o == n_seq - 1:
                        second_level(*placed[o - 1])
                        third_level(*placed[o - 2])
                rows = dl.at[k, rows_at(block * tok, tok)]
                arrived(rows, dl_slots[off, c])
                fwd_slots[off, c] = sems()
                go(rows, rows, fwd_slots[off, c], (mate, v))
            rows = dl.at[1 - k, rows_at(block * tok, tok)]
            arrived(rows, mate_slots[c] if off == 0 else fwd_slots[off, c])
            for jj in range(pairs):

                def put_send(cols, res, o=o, jj=jj):
                    g_send[o, jj, :, cols] = res.astype(bf16)

                def put_keep(cols, res, o=o, jj=jj):
                    g_keep[o, jj, :, cols] = res

                grad_piece(block * tok, 2 * jj + 1 - odd, put_send)
                g_slots[o, jj] = sems()
                go(g_send.at[o, jj], g_recv.at[o, jj], g_slots[o, jj], near)
                grad_piece(block * tok, 2 * jj + odd, put_keep)
    third_level(*placed[n_seq - 2])
    second_level(*placed[n_seq - 1])
    third_level(*placed[n_seq - 1])

    for r in range(n2):

        @pl.when(jnp.logical_not(jnp.logical_and(diagonal_one, quad == r)))
        def _():
            arrived(fin_recv.at[pl.ds(r * share, share)], fin_in + r)

    out[...] = fin_recv[...]
    for o, block in placed:
        for jj in range(pairs):
            t_s, t_v = target(block, jj)

            @pl.when(jnp.logical_not(jnp.logical_and(t_s == s, t_v == v)))
            def _():
                deliver(o, jj, block).wait_send()

    for c in sent:
        c.wait_send()


def per_device(n_seq, n_voc, hidden, head_weight, queries, passage_lengths, pairing, doc_freq):
    tok, width = hidden.shape
    blk, voc = head_weight.shape
    passages, n_q = passage_lengths.shape[0], queries.shape[0]
    chips, half, n2 = n_seq // 2, voc // 2, n_voc // 2
    pairs = n_voc // n_seq // 2
    piece = width // n_voc
    others = max(chips - 1, 1)
    n_sem = 32 + 20 * chips + 3 * n_voc + n2 + n_seq * pairs * (2 * n2 + 2)
    pad = passages + 8
    vmem = pltpu.VMEM
    scratch = [
        vmem((tok, width), bf16),
        vmem((blk, voc), bf16),
        vmem((n_seq * tok, 2 * blk), bf16),
        vmem((blk, half), bf16),
        vmem((others, 2 * tok, half), PART),
        vmem((others, 2 * tok, half), PART),
        vmem((others, 4, half // TILE, tok // 2), f32),
        vmem((others, 4, half // TILE, tok // 2), f32),
        vmem((2 * tok, half), f32),
        vmem((chips, passages, half), f32),
        vmem((passages, half), f32),
        vmem((passages, half), f32),
        vmem((pad, 128), f32),
        vmem((pad, 128), f32),
        vmem((n_voc, pad, 128), f32),
        vmem((2, n_seq * tok, half), bf16),
        vmem((n_seq, pairs, tok, piece), bf16),
        vmem((n_seq, pairs, tok, piece), bf16),
        vmem((n_seq, pairs, tok, piece), f32),
        vmem((n_seq, pairs, tok, piece), bf16),
        vmem((n_seq, pairs, n2, tok // n2, piece), bf16),
        vmem((n_seq, pairs, tok // n2, piece), bf16),
        vmem((tok, piece), bf16),
        pltpu.SemaphoreType.DMA((n_sem,)),
        pltpu.SemaphoreType.DMA((n_sem,)),
        pltpu.SemaphoreType.DMA((2,)),
    ]
    spec = pl.BlockSpec(memory_space=pltpu.VMEM)
    grad, losses = pl.pallas_call(
        functools.partial(kernel, n_seq, n_voc, n_sem),
        out_shape=(
            jax.ShapeDtypeStruct((tok, piece), bf16),
            jax.ShapeDtypeStruct((1, 128), f32),
        ),
        in_specs=[pl.BlockSpec(memory_space=pl.ANY)] * 2 + [spec] * 4,
        out_specs=(spec, spec),
        scratch_shapes=scratch,
        compiler_params=pltpu.CompilerParams(
            collective_id=0, has_side_effects=True, vmem_limit_bytes=56 * 1024 * 1024
        ),
    )(
        hidden, head_weight, queries, passage_lengths[None, :], pairing[None, :],
        doc_freq[None, :],
    )
    return grad, losses[0, :2]


def solution(mesh):
    placed = (P("seq", None), P("seq", "vocab"), P(None, "vocab"), P(), P(), P("vocab"))
    return jax.shard_map(
        functools.partial(per_device, mesh.shape["seq"], mesh.shape["vocab"]),
        mesh=mesh, in_specs=placed, out_specs=(P("seq", "vocab"), P()), check_vma=False,
    )
```
